512 devices in a mesh: space: 16 (over y, x_hi, core), energy: 32 (over z, x_lo).
Axes of the slice: x: 4 (x_hi: 2, x_lo: 2; x = x_hi * 2 + x_lo), y: 4, z: 16, core: 2. Of those that a mesh axis runs over, the one named last changes fastest.
Arguments:
- lesser: bfloat16 [32, 16, 3, 128, 256], P('energy', 'space'), may hold values from -6 to 6
- greater: bfloat16 [32, 16, 3, 128, 256], P('energy', 'space'), may hold values from -1.0546875 to 1.0546875
Outputs:
- polarization: float32 [32, 16, 3, 128, 256], P('energy', 'space')
The draws below stay inside these ranges and needn't reach their ends.
All inputs are finite; a program needn't handle non-finite values.
Results may differ from the reference program's by a relative error of at most 0.0003.
Values may be sent and summed in bfloat16 or wider, within the bound.
A program may use at most 64 MiB of HBM per device.

```python
import jax
import jax.numpy as jnp
from jax import lax

BS = 128
NB = 16
NE = 32


def steps_of(rng, dims, pieces, low, high):
    gain = 1.0
    for position, shards_of in pieces:
        heights = jax.random.uniform(jax.random.fold_in(jax.random.fold_in(rng, 6), position), (shards_of,), jnp.float32, low / len(pieces), high / len(pieces))
        gain = gain * jnp.repeat(jnp.exp(heights), dims[position] // shards_of).reshape((-1,) + (1,) * (len(dims) - 1 - position))
    return gain


def gaussian(rng, dims, spread, most, cuts=(), held_as=jnp.bfloat16):
    loudness = steps_of(rng, dims, cuts, -0.22, 0.18) if cuts else 1.0
    values = jax.random.normal(rng, dims, jnp.float32) * spread * loudness
    return jnp.minimum(jnp.maximum(values, -most), most).astype(held_as)


def setup_inputs(seed: int = 0) -> dict:
    key_of = jax.random.split(jax.random.key(seed), 3)
    return {
        "lesser": gaussian(key_of[0], (NE, NB, 3, BS, 2 * BS), 1.0, 6.0, ((0, 32), (1, 16))),
        "greater": gaussian(key_of[1], (NE, NB, 3, BS, 2 * BS), (NE ** -0.5), 1.0546875, ((0, 32), (1, 16))),
    }


def flip_tiles(tiles):
    shape = tiles.shape
    width = shape[-2]
    split = tiles.reshape(shape[:-1] + (2, width))
    turned = jnp.swapaxes(split, -3, -1)
    return turned.reshape(shape)


def mirror_all(greater):
    zero_tile = jnp.zeros_like(greater[:, :1, 0])
    below = jnp.concatenate([zero_tile, greater[:, :-1, 2]], axis=1)
    above = jnp.concatenate([greater[:, 1:, 0], zero_tile], axis=1)
    stacked = jnp.stack([below, greater[:, :, 1], above], axis=2)
    return flip_tiles(stacked)


def reference(lesser, greater):
    mirrored = mirror_all(greater)
    total = lesser.shape[0]
    width = lesser.shape[3]

    def one_row(pair):
        left, right = pair
        left = left.astype(jnp.float32)
        right = right.astype(jnp.float32)
        left_c = left[..., :width] + 1j * left[..., width:]
        right_c = right[..., :width] + 1j * right[..., width:]
        left_hat = jnp.fft.fft(left_c, axis=0)
        right_hat = jnp.fft.ifft(right_c, axis=0) * total
        result = jnp.fft.ifft(left_hat * right_hat, axis=0)
        return jnp.concatenate([jnp.real(result), jnp.imag(result)], axis=-1).astype(jnp.float32)

    rows = lax.map(one_row, (jnp.swapaxes(lesser, 0, 1), jnp.swapaxes(mirrored, 0, 1)))
    return jnp.swapaxes(rows, 0, 1)
```

```python
import functools
import math

import jax
import jax.numpy as jnp
from jax import lax
from jax.experimental import pallas as pl
from jax.experimental.pallas import tpu as pltpu
from jax.sharding import PartitionSpec as P

MESH = pl.DeviceIdType.MESH
F32 = jnp.float32

BOUND = 405.0 * 1.002
STEEP, SHALLOW, KNEE = 13.2, 5.0, 10.0
TOP = 127.0
SHIFT = (STEEP - SHALLOW) * KNEE


def encode(value, scale):
    part = jnp.abs(value) * scale
    octave = jnp.log2(jnp.maximum(part, 2.0**-33))
    code = jnp.exp2(TOP + jnp.maximum(STEEP * octave, SHALLOW * octave - SHIFT))
    code = jnp.where(part < 2.0**-33, 0.0, code)
    return jnp.where(value < 0, -code, code)


def decode(code, bound):
    size = jnp.abs(code)
    level = jnp.log2(jnp.maximum(size, 2.0**-126)) - TOP
    octave = jnp.minimum(level * (1.0 / STEEP), (level + SHIFT) * (1.0 / SHALLOW))
    value = jnp.exp2(octave) * bound
    value = jnp.where(size == 0, 0.0, value)
    return jnp.where(code < 0, -value, value)


def cadd(a, b):
    return a[0] + b[0], a[1] + b[1]


def csub(a, b):
    return a[0] - b[0], a[1] - b[1]


def turn(a, step, total):
    step = step % total
    eighth = 8 * step
    re, im = a
    if eighth % total == 0:
        way = eighth // total
        if way % 2 == 0:
            return [(re, im), (im, -re), (-re, -im), (-im, re)][way // 2]
        half = math.sqrt(0.5)
        p, m = (re + im) * half, (im - re) * half
        return {1: (p, m), 3: (m, -p), 5: (-p, -m), 7: (-m, p)}[way]
    c = math.cos(2 * math.pi * step / total)
    s = math.sin(2 * math.pi * step / total)
    return re * c + im * s, im * c - re * s


def fft(values, sign):
    n = len(values)
    if n == 1:
        return values
    even, odd = fft(values[0::2], sign), fft(values[1::2], sign)
    odd = [turn(v, sign * k, n) for k, v in enumerate(odd)]
    return [cadd(a, b) for a, b in zip(even, odd)] + [csub(a, b) for a, b in zip(even, odd)]


def kernel(
    n_space, n_energy,
    l_ref, g_ref, o_ref,
    halo, own, mirror, lbuf, gbuf, work, wide, code, back,
    own_sem, halo_send, halo_recv, lsend, gsend, lrecv, grecv, psend, precv,
):
    space, me = lax.axis_index("space"), lax.axis_index("energy")
    core = lax.rem(space, 2)
    plane, side = me // 2, lax.rem(me, 2)
    up, down = lax.rem(space + 1, n_space), lax.rem(space + n_space - 1, n_space)

    def owner(unit):
        late = unit - 16
        z = jnp.where(unit < 16, unit, 4 * (late // 2) + lax.rem(late, 2) + 2 * core)
        x = lax.rem(lax.rem(z, 2) + core + jnp.where(unit < 16, 0, 1), 2)
        return 2 * z + x

    first = side == lax.rem(plane + core, 2)
    rest = lax.rem(plane, 4) - 2 * core
    second = jnp.logical_and(jnp.logical_not(first), jnp.logical_or(rest == 0, rest == 1))
    unit_here = jnp.where(first, plane, 16 + 2 * (plane // 4) + rest)
    works = jnp.logical_or(first, second)

    barrier = pltpu.get_barrier_semaphore()
    pl.semaphore_signal(barrier, inc=1, device_id=(up, me), device_id_type=MESH)
    pl.semaphore_signal(barrier, inc=1, device_id=(down, me), device_id_type=MESH)

    @pl.loop(1, n_energy)
    def _(k):
        pl.semaphore_signal(
            barrier, inc=1, device_id=(space, lax.rem(me + k, n_energy)), device_id_type=MESH
        )

    own_copy = pltpu.make_async_copy(g_ref.at[0, 0, 1], own, own_sem)
    own_copy.start()

    def flipped(tile):
        tile = tile.astype(F32)
        return jnp.concatenate([tile[:, :128].T, tile[:, 128:].T], axis=1)

    own_copy.wait()
    mirror[1] = flipped(own[...]).astype(jnp.bfloat16)
    pl.semaphore_wait(barrier, n_energy + 1)

    halos = [
        pltpu.make_async_remote_copy(
            g_ref.at[0, 0, 2 - 2 * i], halo.at[i], halo_send.at[i], halo_recv.at[i],
            device_id=(dest, me), device_id_type=MESH,
        )
        for i, dest in ((0, up), (1, down))
    ]
    for copy in halos:
        copy.start()

    def unit_rows(unit):
        return unit // 8, pl.ds(pl.multiple_of(lax.rem(unit, 8) * 16, 16), 16)

    def spread(source, target, send, recv, start, count):
        @pl.loop(0, count)
        def _(k):
            unit = start + lax.rem(plane + k, count)
            dest = owner(unit)
            t, rows = unit_rows(unit)

            @pl.when(dest != me)
            def _():
                pltpu.make_async_remote_copy(
                    source.at[t, rows], target.at[me], send.at[unit], recv,
                    device_id=(space, dest), device_id_type=MESH,
                ).start()

            @pl.when(dest == me)
            def _():
                pltpu.make_async_copy(source.at[t, rows], target.at[me], recv).start()

    lesser = l_ref.at[0, 0]
    spread(lesser, lbuf, lsend, lrecv, 0, 16)
    halos[0].wait_recv()
    left = flipped(halo[0])
    mirror[0] = jnp.where(space > 0, left, 0.0).astype(jnp.bfloat16)
    spread(mirror, gbuf, gsend, grecv, 0, 16)
    spread(lesser, lbuf, lsend, lrecv, 16, 8)
    halos[1].wait_recv()
    right = flipped(halo[1])
    mirror[2] = jnp.where(space < n_space - 1, right, 0.0).astype(jnp.bfloat16)
    spread(mirror, gbuf, gsend, grecv, 16, 8)

    scale = 1.0 / (n_energy * BOUND)

    @pl.when(works)
    def _():
        pltpu.make_async_copy(lbuf, lbuf, lrecv).wait()
        pltpu.make_async_copy(gbuf, gbuf, grecv).wait()

        def read(ref, e):
            pair = ref[e].astype(F32)
            return pair[:, :128], pair[:, 128:]

        for part, (ref, sign) in enumerate(((lbuf, 1), (gbuf, -1))):
            for r in range(4):
                out = fft([read(ref, 4 * a + r) for a in range(8)], sign)
                for s, v in enumerate(out):
                    v = turn(v, sign * r * s, 32)
                    work[part, 4 * s + r, :, :128] = v[0]
                    work[part, 4 * s + r, :, 128:] = v[1]
        for s in range(8):
            hats = []
            for part, sign in ((0, 1), (1, -1)):
                pairs = [
                    (work[part, 4 * s + r, :, :128], work[part, 4 * s + r, :, 128:]) for r in range(4)
                ]
                hats.append(fft(pairs, sign))
            prods = [
                (a[0] * b[0] - a[1] * b[1], a[0] * b[1] + a[1] * b[0]) for a, b in zip(*hats)
            ]
            for r, v in enumerate(fft(prods, -1)):
                v = turn(v, -r * s, 32)
                wide[8 * r + s, :, :128] = v[0]
                wide[8 * r + s, :, 128:] = v[1]
        for r in range(4):
            pairs = [(wide[8 * r + s, :, :128], wide[8 * r + s, :, 128:]) for s in range(8)]
            for a, v in enumerate(fft(pairs, -1)):
                code[4 * a + r] = encode(jnp.concatenate(v, axis=1), scale).astype(jnp.bfloat16)

        @pl.loop(1, n_energy)
        def _(k):
            dest = lax.rem(me + k, n_energy)
            pltpu.make_async_remote_copy(
                code.at[dest], back.at[unit_here], psend.at[dest], precv.at[unit_here],
                device_id=(space, dest), device_id_type=MESH,
            ).start()

        pltpu.make_async_copy(code.at[me], back.at[unit_here], precv.at[unit_here]).start()

    @pl.loop(0, 24)
    def _(k):
        unit = jnp.where(k < 16, lax.rem(plane + k, 16), k)
        t, rows = unit_rows(unit)
        pltpu.make_async_copy(back.at[unit], back.at[unit], precv.at[unit]).wait()
        o_ref[0, 0, t, rows, :] = decode(back[unit].astype(F32), BOUND)

    for copy in halos:
        copy.wait_send()

    @pl.loop(0, 24)
    def _(unit):
        dest = owner(unit)

        @pl.when(dest != me)
        def _():
            for source, send in ((lbuf, lsend), (gbuf, gsend)):
                pltpu.make_async_copy(source.at[0], source.at[0], send.at[unit]).wait()

    @pl.when(works)
    def _():
        @pl.loop(1, n_energy)
        def _(k):
            dest = lax.rem(me + k, n_energy)
            pltpu.make_async_copy(code.at[dest], code.at[dest], psend.at[dest]).wait()


def on_device(n_space, n_energy, lesser, greater):
    unit = (16, 256)
    dma = pltpu.SemaphoreType.DMA
    return pl.pallas_call(
        functools.partial(kernel, n_space, n_energy),
        out_shape=jax.ShapeDtypeStruct(lesser.shape, F32),
        in_specs=[pl.BlockSpec(memory_space=pltpu.HBM)] * 2,
        out_specs=pl.BlockSpec(memory_space=pltpu.VMEM),
        scratch_shapes=[
            pltpu.VMEM((2, 128, 256), jnp.bfloat16),
            pltpu.VMEM((128, 256), jnp.bfloat16),
            pltpu.VMEM((3, 128, 256), jnp.bfloat16),
            pltpu.VMEM((n_energy, *unit), jnp.bfloat16),
            pltpu.VMEM((n_energy, *unit), jnp.bfloat16),
            pltpu.VMEM((2, n_energy, *unit), F32),
            pltpu.VMEM((n_energy, *unit), F32),
            pltpu.VMEM((n_energy, *unit), jnp.bfloat16),
            pltpu.VMEM((24, *unit), jnp.bfloat16),
            dma,
            dma((2,)),
            dma((2,)),
            dma((24,)),
            dma((24,)),
            dma,
            dma,
            dma((n_energy,)),
            dma((24,)),
        ],
        compiler_params=pltpu.CompilerParams(
            collective_id=0, has_side_effects=True, vmem_limit_bytes=32 << 20
        ),
    )(lesser, greater)


def solution(mesh):
    spec = P("energy", "space", None, None, None)
    return jax.shard_map(
        functools.partial(on_device, mesh.shape["space"], mesh.shape["energy"]),
        mesh=mesh,
        in_specs=(spec, spec),
        out_specs=spec,
        check_vma=False,
    )
```

```python
import functools
import math

import jax
import jax.numpy as jnp
from jax import lax
from jax.experimental import pallas as pl
from jax.experimental.pallas import tpu as pltpu
from jax.sharding import PartitionSpec as P

MESH = pl.DeviceIdType.MESH
F32 = jnp.float32

BOUND = 405.0 * 1.002
STEEP, SHALLOW, KNEE = 13.2, 5.0, 10.0
TOP = 127.0
SHIFT = (STEEP - SHALLOW) * KNEE


def encode(value, scale):
    part = jnp.abs(value) * scale
    octave = jnp.log2(jnp.maximum(part, 2.0**-33))
    code = jnp.exp2(TOP + jnp.maximum(STEEP * octave, SHALLOW * octave - SHIFT))
    code = jnp.where(part < 2.0**-33, 0.0, code)
    return jnp.where(value < 0, -code, code)


def decode(code, bound):
    size = jnp.abs(code)
    level = jnp.log2(jnp.maximum(size, 2.0**-126)) - TOP
    octave = jnp.minimum(level * (1.0 / STEEP), (level + SHIFT) * (1.0 / SHALLOW))
    value = jnp.exp2(octave) * bound
    value = jnp.where(size == 0, 0.0, value)
    return jnp.where(code < 0, -value, value)


def cadd(a, b):
    return a[0] + b[0], a[1] + b[1]


def csub(a, b):
    return a[0] - b[0], a[1] - b[1]


def turn(a, step, total):
    step = step % total
    eighth = 8 * step
    re, im = a
    if eighth % total == 0:
        way = eighth // total
        if way % 2 == 0:
            return [(re, im), (im, -re), (-re, -im), (-im, re)][way // 2]
        half = math.sqrt(0.5)
        p, m = (re + im) * half, (im - re) * half
        return {1: (p, m), 3: (m, -p), 5: (-p, -m), 7: (-m, p)}[way]
    c = math.cos(2 * math.pi * step / total)
    s = math.sin(2 * math.pi * step / total)
    return re * c + im * s, im * c - re * s


def fft(values, sign):
    n = len(values)
    if n == 1:
        return values
    even, odd = fft(values[0::2], sign), fft(values[1::2], sign)
    odd = [turn(v, sign * k, n) for k, v in enumerate(odd)]
    return [cadd(a, b) for a, b in zip(even, odd)] + [csub(a, b) for a, b in zip(even, odd)]


def kernel(
    n_space, n_energy,
    l_ref, g_ref, o_ref,
    halo, local, mirror, lbuf, gbuf, work, wide, code,
    own_sem, halo_send, halo_recv, lsend, gsend, lrecv, grecv, psend, precv,
):
    space, me = lax.axis_index("space"), lax.axis_index("energy")
    core = lax.rem(space, 2)
    plane, side = me // 2, lax.rem(me, 2)
    up, down = lax.rem(space + 1, n_space), lax.rem(space + n_space - 1, n_space)

    first = side == lax.rem(plane + core, 2)
    rest = lax.rem(plane, 4) - 2 * core
    second = jnp.logical_and(jnp.logical_not(first), jnp.logical_or(rest == 0, rest == 1))
    unit_here = jnp.where(first, plane, 16 + 2 * (plane // 4) + rest)
    works = jnp.logical_or(first, second)

    l_copy = pltpu.make_async_copy(l_ref.at[0, 0], local.at[pl.ds(0, 3)], own_sem.at[0])
    own_copy = pltpu.make_async_copy(g_ref.at[0, 0, 1], local.at[3], own_sem.at[1])
    l_copy.start()
    own_copy.start()
    barrier = pltpu.get_barrier_semaphore()
    pl.semaphore_signal(barrier, inc=1, device_id=(up, me), device_id_type=MESH)
    pl.semaphore_signal(barrier, inc=1, device_id=(down, me), device_id_type=MESH)

    @pl.loop(1, n_energy)
    def _(k):
        pl.semaphore_signal(
            barrier, inc=1, device_id=(space, lax.rem(me + k, n_energy)), device_id_type=MESH
        )

    def flipped(tile):
        tile = tile.astype(F32)
        return jnp.concatenate([tile[:, :128].T, tile[:, 128:].T], axis=1)

    pl.semaphore_wait(barrier, n_energy + 1)

    halos = [
        pltpu.make_async_remote_copy(
            g_ref.at[0, 0, 2 - 2 * i], halo.at[i], halo_send.at[i], halo_recv.at[i],
            device_id=(dest, me), device_id_type=MESH,
        )
        for i, dest in ((0, up), (1, down))
    ]
    for copy in halos:
        copy.start()

    def unit_rows(unit):
        return unit // 8, pl.ds(pl.multiple_of(lax.rem(unit, 8) * 16, 16), 16)

    def plane_at(k):
        away = 8 + jnp.where(lax.rem(k, 2) == 0, k // 2, -((k + 1) // 2))
        return lax.rem(plane + away, 16)

    def has_second(z):
        late = lax.rem(z, 4) - 2 * core
        return jnp.logical_or(late == 0, late == 1)

    def unit_of(z, which):
        return z if which == 0 else 16 + 2 * (z // 4) + lax.rem(lax.rem(z, 4), 2)

    def owner_of(z, which):
        return 2 * z + lax.rem(lax.rem(z, 2) + core + which, 2)

    def send(source, target, sems, recv, z, which):
        unit, dest = unit_of(z, which), owner_of(z, which)
        t, rows = unit_rows(unit)

        @pl.when(dest != me)
        def _():
            pltpu.make_async_remote_copy(
                source.at[t, rows], target.at[me], sems.at[unit], recv,
                device_id=(space, dest), device_id_type=MESH,
            ).start()

        @pl.when(dest == me)
        def _():
            pltpu.make_async_copy(source.at[t, rows], target.at[me], recv).start()

    def sent(source, sems, z, which):
        @pl.when(owner_of(z, which) != me)
        def _():
            pltpu.make_async_copy(source.at[0], source.at[0], sems.at[unit_of(z, which)]).wait()

    l_copy.wait()

    @pl.loop(0, 16)
    def _(k):
        z = plane_at(k)
        send(local, lbuf, lsend, lrecv, z, 0)

        @pl.when(has_second(z))
        def _():
            send(local, lbuf, lsend, lrecv, z, 1)

    own_copy.wait()
    mirror[1] = flipped(local[3]).astype(jnp.bfloat16)
    halos[0].wait_recv()
    left = flipped(halo[0])
    mirror[0] = jnp.where(space > 0, left, 0.0).astype(jnp.bfloat16)
    halos[1].wait_recv()
    right = flipped(halo[1])
    mirror[2] = jnp.where(space < n_space - 1, right, 0.0).astype(jnp.bfloat16)

    @pl.loop(0, 16)
    def _(k):
        z = plane_at(k)
        sent(lbuf, lsend, z, 0)
        send(mirror, gbuf, gsend, grecv, z, 0)

        @pl.when(has_second(z))
        def _():
            sent(lbuf, lsend, z, 1)
            send(mirror, gbuf, gsend, grecv, z, 1)

    @pl.loop(0, 16)
    def _(k):
        sent(gbuf, gsend, plane_at(k), 0)

    scale = 1.0 / (n_energy * BOUND)

    @pl.when(works)
    def _():
        pltpu.make_async_copy(lbuf, lbuf, lrecv).wait()
        pltpu.make_async_copy(gbuf, gbuf, grecv).wait()

        def read(ref, e):
            pair = ref[e].astype(F32)
            return pair[:, :128], pair[:, 128:]

        for part, (ref, sign) in enumerate(((lbuf, 1), (gbuf, -1))):
            for r in range(4):
                out = fft([read(ref, 4 * a + r) for a in range(8)], sign)
                for s, v in enumerate(out):
                    v = turn(v, sign * r * s, 32)
                    work[part, 4 * s + r, :, :128] = v[0]
                    work[part, 4 * s + r, :, 128:] = v[1]
        for s in range(8):
            hats = []
            for part, sign in ((0, 1), (1, -1)):
                pairs = [
                    (work[part, 4 * s + r, :, :128], work[part, 4 * s + r, :, 128:]) for r in range(4)
                ]
                hats.append(fft(pairs, sign))
            prods = [
                (a[0] * b[0] - a[1] * b[1], a[0] * b[1] + a[1] * b[0]) for a, b in zip(*hats)
            ]
            for r, v in enumerate(fft(prods, -1)):
                v = turn(v, -r * s, 32)
                wide[8 * r + s, :, :128] = v[0]
                wide[8 * r + s, :, 128:] = v[1]
        for r in range(4):
            pairs = [(wide[8 * r + s, :, :128], wide[8 * r + s, :, 128:]) for s in range(8)]
            for a, v in enumerate(fft(pairs, -1)):
                code[4 * a + r] = encode(jnp.concatenate(v, axis=1), scale).astype(jnp.bfloat16)

        def give(dest):
            @pl.when(dest != me)
            def _():
                pltpu.make_async_remote_copy(
                    code.at[dest], o_ref.at[unit_here], psend.at[dest], precv.at[unit_here],
                    device_id=(space, dest), device_id_type=MESH,
                ).start()

            @pl.when(dest == me)
            def _():
                pltpu.make_async_copy(code.at[dest], o_ref.at[unit_here], precv.at[unit_here]).start()

        @pl.loop(0, 32)
        def _(k):
            give(k)

    @pl.loop(0, 24)
    def _(k):
        pltpu.make_async_copy(o_ref.at[k], o_ref.at[k], precv.at[k]).wait()

    for copy in halos:
        copy.wait_send()

    @pl.loop(0, 16)
    def _(z):
        @pl.when(has_second(z))
        def _():
            sent(gbuf, gsend, z, 1)

    @pl.when(works)
    def _():
        @pl.loop(1, n_energy)
        def _(k):
            dest = lax.rem(me + k, n_energy)
            pltpu.make_async_copy(code.at[dest], code.at[dest], psend.at[dest]).wait()


def on_device(n_space, n_energy, lesser, greater):
    unit = (16, 256)
    dma = pltpu.SemaphoreType.DMA
    codes = pl.pallas_call(
        functools.partial(kernel, n_space, n_energy),
        out_shape=pltpu.VMEM((24, *unit), jnp.bfloat16),
        in_specs=[pl.BlockSpec(memory_space=pltpu.HBM)] * 2,
        out_specs=pl.BlockSpec(memory_space=pltpu.VMEM),
        scratch_shapes=[
            pltpu.VMEM((2, 128, 256), jnp.bfloat16),
            pltpu.VMEM((4, 128, 256), jnp.bfloat16),
            pltpu.VMEM((3, 128, 256), jnp.bfloat16),
            pltpu.VMEM((n_energy, *unit), jnp.bfloat16),
            pltpu.VMEM((n_energy, *unit), jnp.bfloat16),
            pltpu.VMEM((2, n_energy, *unit), F32),
            pltpu.VMEM((n_energy, *unit), F32),
            pltpu.VMEM((n_energy, *unit), jnp.bfloat16),
            dma((2,)),
            dma((2,)),
            dma((2,)),
            dma((24,)),
            dma((24,)),
            dma,
            dma,
            dma((n_energy,)),
            dma((24,)),
        ],
        compiler_params=pltpu.CompilerParams(
            collective_id=0, has_side_effects=True, vmem_limit_bytes=62 << 20
        ),
    )(lesser, greater)
    return decode(codes.reshape(lesser.shape).astype(F32), BOUND)


def solution(mesh):
    spec = P("energy", "space", None, None, None)
    return jax.shard_map(
        functools.partial(on_device, mesh.shape["space"], mesh.shape["energy"]),
        mesh=mesh,
        in_specs=(spec, spec),
        out_specs=spec,
        check_vma=False,
    )
```

```python
import functools
import math

import jax
import jax.numpy as jnp
from jax import lax
from jax.experimental import pallas as pl
from jax.experimental.pallas import tpu as pltpu
from jax.sharding import PartitionSpec as P

MESH = pl.DeviceIdType.MESH
REACH, STEPS = 4, 1
F32 = jnp.float32

BOUND = 405.0 * 1.002
STEEP, SHALLOW, KNEE = 13.2, 5.0, 10.0
TOP = 127.0
SHIFT = (STEEP - SHALLOW) * KNEE


def encode(value, scale):
    part = jnp.abs(value) * scale
    octave = jnp.log2(jnp.maximum(part, 2.0**-33))
    code = jnp.exp2(TOP + jnp.maximum(STEEP * octave, SHALLOW * octave - SHIFT))
    code = jnp.where(part < 2.0**-33, 0.0, code)
    return jnp.where(value < 0, -code, code)


def decode(code, bound):
    size = jnp.abs(code)
    level = jnp.log2(jnp.maximum(size, 2.0**-126)) - TOP
    octave = jnp.minimum(level * (1.0 / STEEP), (level + SHIFT) * (1.0 / SHALLOW))
    value = jnp.exp2(octave) * bound
    value = jnp.where(size == 0, 0.0, value)
    return jnp.where(code < 0, -value, value)


def cadd(a, b):
    return a[0] + b[0], a[1] + b[1]


def csub(a, b):
    return a[0] - b[0], a[1] - b[1]


def turn(a, step, total):
    step = step % total
    eighth = 8 * step
    re, im = a
    if eighth % total == 0:
        way = eighth // total
        if way % 2 == 0:
            return [(re, im), (im, -re), (-re, -im), (-im, re)][way // 2]
        half = math.sqrt(0.5)
        p, m = (re + im) * half, (im - re) * half
        return {1: (p, m), 3: (m, -p), 5: (-p, -m), 7: (-m, p)}[way]
    c = math.cos(2 * math.pi * step / total)
    s = math.sin(2 * math.pi * step / total)
    return re * c + im * s, im * c - re * s


def fft(values, sign):
    n = len(values)
    if n == 1:
        return values
    even, odd = fft(values[0::2], sign), fft(values[1::2], sign)
    odd = [turn(v, sign * k, n) for k, v in enumerate(odd)]
    return [cadd(a, b) for a, b in zip(even, odd)] + [csub(a, b) for a, b in zip(even, odd)]


def kernel(
    n_space, n_energy,
    l_ref, g_ref, o_ref,
    halo, local, mirror, lbuf, gbuf, work, wide, code,
    own_sem, halo_send, halo_recv, lsend, gsend, lrecv, grecv, psend, precv, from_behind, from_ahead,
):
    space, me = lax.axis_index("space"), lax.axis_index("energy")
    core = lax.rem(space, 2)
    plane, side = me // 2, lax.rem(me, 2)
    up, down = lax.rem(space + 1, n_space), lax.rem(space + n_space - 1, n_space)

    first = side == lax.rem(plane + core, 2)
    rest = lax.rem(plane, 4) - 2 * core
    second = jnp.logical_and(jnp.logical_not(first), jnp.logical_or(rest == 0, rest == 1))
    unit_here = jnp.where(first, plane, 16 + 2 * (plane // 4) + rest)
    works = jnp.logical_or(first, second)

    l_copy = pltpu.make_async_copy(l_ref.at[0, 0], local.at[pl.ds(0, 3)], own_sem.at[0])
    own_copy = pltpu.make_async_copy(g_ref.at[0, 0, 1], local.at[3], own_sem.at[1])
    l_copy.start()
    own_copy.start()
    barrier = pltpu.get_barrier_semaphore()
    pl.semaphore_signal(barrier, inc=1, device_id=(up, me), device_id_type=MESH)
    pl.semaphore_signal(barrier, inc=1, device_id=(down, me), device_id_type=MESH)


    @pl.loop(0, 2 * (2 * REACH + 1))
    def _(k):
        peer = lax.rem(2 * plane + n_energy - 2 * REACH + k, n_energy)

        @pl.when(peer != me)
        def _():
            pl.semaphore_signal(barrier, inc=1, device_id=(space, peer), device_id_type=MESH)

    ahead = (space, lax.rem(me + 2 * REACH, n_energy))
    behind = (space, lax.rem(me + n_energy - 2 * REACH, n_energy))

    def flipped(tile):
        tile = tile.astype(F32)
        return jnp.concatenate([tile[:, :128].T, tile[:, 128:].T], axis=1)

    pl.semaphore_wait(barrier, 2 * (2 * REACH + 1) + 1)

    def tell(sem, peer):
        pl.semaphore_signal(sem, inc=1, device_id=peer, device_id_type=MESH)

    tell(from_behind.at[1], ahead)
    tell(from_ahead.at[1], behind)

    halos = [
        pltpu.make_async_remote_copy(
            g_ref.at[0, 0, 2 - 2 * i], halo.at[i], halo_send.at[i], halo_recv.at[i],
            device_id=(dest, me), device_id_type=MESH,
        )
        for i, dest in ((0, up), (1, down))
    ]
    for copy in halos:
        copy.start()

    def unit_rows(unit):
        return unit // 8, pl.ds(pl.multiple_of(lax.rem(unit, 8) * 16, 16), 16)

    def plane_at(k):
        away = 8 + jnp.where(lax.rem(k, 2) == 0, k // 2, -((k + 1) // 2))
        return lax.rem(plane + away, 16)

    def has_second(z):
        late = lax.rem(z, 4) - 2 * core
        return jnp.logical_or(late == 0, late == 1)

    def unit_of(z, which):
        return z if which == 0 else 16 + 2 * (z // 4) + lax.rem(lax.rem(z, 4), 2)

    def owner_of(z, which):
        return 2 * z + lax.rem(lax.rem(z, 2) + core + which, 2)

    def send(source, target, sems, recv, z, which):
        unit, dest = unit_of(z, which), owner_of(z, which)
        t, rows = unit_rows(unit)

        @pl.when(dest != me)
        def _():
            pltpu.make_async_remote_copy(
                source.at[t, rows], target.at[me], sems.at[unit], recv,
                device_id=(space, dest), device_id_type=MESH,
            ).start()

        @pl.when(dest == me)
        def _():
            pltpu.make_async_copy(source.at[t, rows], target.at[me], recv).start()

    def sent(source, sems, z, which):
        @pl.when(owner_of(z, which) != me)
        def _():
            pltpu.make_async_copy(source.at[0], source.at[0], sems.at[unit_of(z, which)]).wait()

    l_copy.wait()

    def send_lesser(z):
        send(local, lbuf, lsend, lrecv, z, 0)

        @pl.when(has_second(z))
        def _():
            send(local, lbuf, lsend, lrecv, z, 1)

    def send_greater(z):
        send(mirror, gbuf, gsend, grecv, z, 0)

        @pl.when(has_second(z))
        def _():
            send(mirror, gbuf, gsend, grecv, z, 1)

    def around(act, distances):
        for k in distances:
            act(lax.rem(plane + 16 - k, 16))
            if k % 8:
                act(lax.rem(plane + k, 16))

    def hear(step):
        for sem, peer in ((from_behind, ahead), (from_ahead, behind)):
            pl.semaphore_wait(sem.at[step], 1)
            if step < STEPS:
                tell(sem.at[step + 1], peer)

    around(send_lesser, (4, 3, 2, 1, 0))
    hear(1)
    around(send_lesser, (8, 7, 6, 5))
    own_copy.wait()
    mirror[1] = flipped(local[3]).astype(jnp.bfloat16)
    halos[0].wait_recv()
    left = flipped(halo[0])
    mirror[0] = jnp.where(space > 0, left, 0.0).astype(jnp.bfloat16)
    halos[1].wait_recv()
    right = flipped(halo[1])
    mirror[2] = jnp.where(space < n_space - 1, right, 0.0).astype(jnp.bfloat16)
    around(send_greater, (8, 7, 6, 5, 4, 3, 2, 1, 0))

    scale = 1.0 / (n_energy * BOUND)

    @pl.when(works)
    def _():
        pltpu.make_async_copy(lbuf, lbuf, lrecv).wait()
        pltpu.make_async_copy(gbuf, gbuf, grecv).wait()

        def read(ref, e):
            pair = ref[e].astype(F32)
            return pair[:, :128], pair[:, 128:]

        for part, (ref, sign) in enumerate(((lbuf, 1), (gbuf, -1))):
            for r in range(4):
                out = fft([read(ref, 4 * a + r) for a in range(8)], sign)
                for s, v in enumerate(out):
                    v = turn(v, sign * r * s, 32)
                    work[part, 4 * s + r, :, :128] = v[0]
                    work[part, 4 * s + r, :, 128:] = v[1]
        for s in range(8):
            hats = []
            for part, sign in ((0, 1), (1, -1)):
                pairs = [
                    (work[part, 4 * s + r, :, :128], work[part, 4 * s + r, :, 128:]) for r in range(4)
                ]
                hats.append(fft(pairs, sign))
            prods = [
                (a[0] * b[0] - a[1] * b[1], a[0] * b[1] + a[1] * b[0]) for a, b in zip(*hats)
            ]
            for r, v in enumerate(fft(prods, -1)):
                v = turn(v, -r * s, 32)
                wide[8 * r + s, :, :128] = v[0]
                wide[8 * r + s, :, 128:] = v[1]
        for r in range(4):
            pairs = [(wide[8 * r + s, :, :128], wide[8 * r + s, :, 128:]) for s in range(8)]
            for a, v in enumerate(fft(pairs, -1)):
                code[4 * a + r] = encode(jnp.concatenate(v, axis=1), scale).astype(jnp.bfloat16)

        def give(dest):
            @pl.when(dest != me)
            def _():
                pltpu.make_async_remote_copy(
                    code.at[dest], o_ref.at[unit_here], psend.at[dest], precv.at[unit_here],
                    device_id=(space, dest), device_id_type=MESH,
                ).start()

            @pl.when(dest == me)
            def _():
                pltpu.make_async_copy(code.at[dest], o_ref.at[unit_here], precv.at[unit_here]).start()

        @pl.loop(0, 32)
        def _(k):
            give(k)

    @pl.loop(0, 24)
    def _(k):
        pltpu.make_async_copy(o_ref.at[k], o_ref.at[k], precv.at[k]).wait()

    for copy in halos:
        copy.wait_send()

    @pl.loop(0, 16)
    def _(z):
        sent(lbuf, lsend, z, 0)
        sent(gbuf, gsend, z, 0)

        @pl.when(has_second(z))
        def _():
            sent(lbuf, lsend, z, 1)
            sent(gbuf, gsend, z, 1)

    @pl.when(works)
    def _():
        @pl.loop(1, n_energy)
        def _(k):
            dest = lax.rem(me + k, n_energy)
            pltpu.make_async_copy(code.at[dest], code.at[dest], psend.at[dest]).wait()


def on_device(n_space, n_energy, lesser, greater):
    unit = (16, 256)
    dma = pltpu.SemaphoreType.DMA
    codes = pl.pallas_call(
        functools.partial(kernel, n_space, n_energy),
        out_shape=pltpu.VMEM((24, *unit), jnp.bfloat16),
        in_specs=[pl.BlockSpec(memory_space=pltpu.HBM)] * 2,
        out_specs=pl.BlockSpec(memory_space=pltpu.VMEM),
        scratch_shapes=[
            pltpu.VMEM((2, 128, 256), jnp.bfloat16),
            pltpu.VMEM((4, 128, 256), jnp.bfloat16),
            pltpu.VMEM((3, 128, 256), jnp.bfloat16),
            pltpu.VMEM((n_energy, *unit), jnp.bfloat16),
            pltpu.VMEM((n_energy, *unit), jnp.bfloat16),
            pltpu.VMEM((2, n_energy, *unit), F32),
            pltpu.VMEM((n_energy, *unit), F32),
            pltpu.VMEM((n_energy, *unit), jnp.bfloat16),
            dma((2,)),
            dma((2,)),
            dma((2,)),
            dma((24,)),
            dma((24,)),
            dma,
            dma,
            dma((n_energy,)),
            dma((24,)),
            pltpu.SemaphoreType.REGULAR((9,)),
            pltpu.SemaphoreType.REGULAR((9,)),
        ],
        compiler_params=pltpu.CompilerParams(
            collective_id=0, has_side_effects=True, vmem_limit_bytes=62 << 20
        ),
    )(lesser, greater)
    return decode(codes.reshape(lesser.shape).astype(F32), BOUND)


def solution(mesh):
    spec = P("energy", "space", None, None, None)
    return jax.shard_map(
        functools.partial(on_device, mesh.shape["space"], mesh.shape["energy"]),
        mesh=mesh,
        in_specs=(spec, spec),
        out_specs=spec,
        check_vma=False,
    )
```

```python
import functools
import math

import jax
import jax.numpy as jnp
from jax import lax
from jax.experimental import pallas as pl
from jax.experimental.pallas import tpu as pltpu
from jax.sharding import PartitionSpec as P

MESH = pl.DeviceIdType.MESH
REACH, STEPS = 4, 1
F32 = jnp.float32

MARGIN = 64.2
STEEP, SHALLOW, KNEE = 13.2, 5.0, 10.0
TOP = 127.0
SHIFT = (STEEP - SHALLOW) * KNEE


def encode(value, scale):
    part = jnp.abs(value) * scale
    octave = jnp.log2(jnp.maximum(part, 2.0**-33))
    code = jnp.exp2(TOP + jnp.maximum(STEEP * octave, SHALLOW * octave - SHIFT))
    code = jnp.where(part < 2.0**-33, 0.0, code)
    return jnp.where(value < 0, -code, code)


def decode(code, bound):
    size = jnp.abs(code)
    level = jnp.log2(jnp.maximum(size, 2.0**-126)) - TOP
    octave = jnp.minimum(level * (1.0 / STEEP), (level + SHIFT) * (1.0 / SHALLOW))
    value = jnp.exp2(octave) * bound
    value = jnp.where(size == 0, 0.0, value)
    return jnp.where(code < 0, -value, value)


def cadd(a, b):
    return a[0] + b[0], a[1] + b[1]


def csub(a, b):
    return a[0] - b[0], a[1] - b[1]


def turn(a, step, total):
    step = step % total
    eighth = 8 * step
    re, im = a
    if eighth % total == 0:
        way = eighth // total
        if way % 2 == 0:
            return [(re, im), (im, -re), (-re, -im), (-im, re)][way // 2]
        half = math.sqrt(0.5)
        p, m = (re + im) * half, (im - re) * half
        return {1: (p, m), 3: (m, -p), 5: (-p, -m), 7: (-m, p)}[way]
    c = math.cos(2 * math.pi * step / total)
    s = math.sin(2 * math.pi * step / total)
    return re * c + im * s, im * c - re * s


def fft(values, sign):
    n = len(values)
    if n == 1:
        return values
    even, odd = fft(values[0::2], sign), fft(values[1::2], sign)
    odd = [turn(v, sign * k, n) for k, v in enumerate(odd)]
    return [cadd(a, b) for a, b in zip(even, odd)] + [csub(a, b) for a, b in zip(even, odd)]


def kernel(
    n_space, n_energy,
    l_ref, g_ref, o_ref,
    halo, local, mirror, lbuf, gbuf, work, wide, code, back, bound_out, bound_in,
    own_sem, halo_send, halo_recv, lsend, gsend, lrecv, grecv, psend, precv, bsend, brecv, from_behind, from_ahead,
):
    space, me = lax.axis_index("space"), lax.axis_index("energy")
    core = lax.rem(space, 2)
    plane, side = me // 2, lax.rem(me, 2)
    up, down = lax.rem(space + 1, n_space), lax.rem(space + n_space - 1, n_space)

    first = side == lax.rem(plane + core, 2)
    rest = lax.rem(plane, 4) - 2 * core
    second = jnp.logical_and(jnp.logical_not(first), jnp.logical_or(rest == 0, rest == 1))
    unit_here = jnp.where(first, plane, 16 + 2 * (plane // 4) + rest)
    works = jnp.logical_or(first, second)

    l_copy = pltpu.make_async_copy(l_ref.at[0, 0], local.at[pl.ds(0, 3)], own_sem.at[0])
    own_copy = pltpu.make_async_copy(g_ref.at[0, 0, 1], local.at[3], own_sem.at[1])
    l_copy.start()
    own_copy.start()
    barrier = pltpu.get_barrier_semaphore()
    pl.semaphore_signal(barrier, inc=1, device_id=(up, me), device_id_type=MESH)
    pl.semaphore_signal(barrier, inc=1, device_id=(down, me), device_id_type=MESH)


    @pl.loop(0, 2 * (2 * REACH + 1))
    def _(k):
        peer = lax.rem(2 * plane + n_energy - 2 * REACH + k, n_energy)

        @pl.when(peer != me)
        def _():
            pl.semaphore_signal(barrier, inc=1, device_id=(space, peer), device_id_type=MESH)

    ahead = (space, lax.rem(me + 2 * REACH, n_energy))
    behind = (space, lax.rem(me + n_energy - 2 * REACH, n_energy))

    def flipped(tile):
        tile = tile.astype(F32)
        return jnp.concatenate([tile[:, :128].T, tile[:, 128:].T], axis=1)

    pl.semaphore_wait(barrier, 2 * (2 * REACH + 1) + 1)

    def tell(sem, peer):
        pl.semaphore_signal(sem, inc=1, device_id=peer, device_id_type=MESH)

    tell(from_behind.at[1], ahead)
    tell(from_ahead.at[1], behind)

    halos = [
        pltpu.make_async_remote_copy(
            g_ref.at[0, 0, 2 - 2 * i], halo.at[i], halo_send.at[i], halo_recv.at[i],
            device_id=(dest, me), device_id_type=MESH,
        )
        for i, dest in ((0, up), (1, down))
    ]
    for copy in halos:
        copy.start()

    def unit_rows(unit):
        return unit // 8, pl.ds(pl.multiple_of(lax.rem(unit, 8) * 16, 16), 16)

    def plane_at(k):
        away = 8 + jnp.where(lax.rem(k, 2) == 0, k // 2, -((k + 1) // 2))
        return lax.rem(plane + away, 16)

    def has_second(z):
        late = lax.rem(z, 4) - 2 * core
        return jnp.logical_or(late == 0, late == 1)

    def unit_of(z, which):
        return z if which == 0 else 16 + 2 * (z // 4) + lax.rem(lax.rem(z, 4), 2)

    def owner_of(z, which):
        return 2 * z + lax.rem(lax.rem(z, 2) + core + which, 2)

    def send(source, target, sems, recv, z, which):
        unit, dest = unit_of(z, which), owner_of(z, which)
        t, rows = unit_rows(unit)

        @pl.when(dest != me)
        def _():
            pltpu.make_async_remote_copy(
                source.at[t, rows], target.at[me], sems.at[unit], recv,
                device_id=(space, dest), device_id_type=MESH,
            ).start()

        @pl.when(dest == me)
        def _():
            pltpu.make_async_copy(source.at[t, rows], target.at[me], recv).start()

    def sent(source, sems, z, which):
        @pl.when(owner_of(z, which) != me)
        def _():
            pltpu.make_async_copy(source.at[0], source.at[0], sems.at[unit_of(z, which)]).wait()

    l_copy.wait()

    def send_lesser(z):
        send(local, lbuf, lsend, lrecv, z, 0)

        @pl.when(has_second(z))
        def _():
            send(local, lbuf, lsend, lrecv, z, 1)

    def send_greater(z):
        send(mirror, gbuf, gsend, grecv, z, 0)

        @pl.when(has_second(z))
        def _():
            send(mirror, gbuf, gsend, grecv, z, 1)

    def around(act, distances):
        for k in distances:
            act(lax.rem(plane + 16 - k, 16))
            if k % 8:
                act(lax.rem(plane + k, 16))

    def hear(step):
        for sem, peer in ((from_behind, ahead), (from_ahead, behind)):
            pl.semaphore_wait(sem.at[step], 1)
            if step < STEPS:
                tell(sem.at[step + 1], peer)

    around(send_lesser, (4, 3, 2, 1, 0))
    hear(1)
    around(send_lesser, (8, 7, 6, 5))
    own_copy.wait()
    mirror[1] = flipped(local[3]).astype(jnp.bfloat16)
    halos[0].wait_recv()
    left = flipped(halo[0])
    mirror[0] = jnp.where(space > 0, left, 0.0).astype(jnp.bfloat16)
    halos[1].wait_recv()
    right = flipped(halo[1])
    mirror[2] = jnp.where(space < n_space - 1, right, 0.0).astype(jnp.bfloat16)
    around(send_greater, (8, 7, 6, 5, 4, 3, 2, 1, 0))

    @pl.when(works)
    def _():
        pltpu.make_async_copy(lbuf, lbuf, lrecv).wait()
        pltpu.make_async_copy(gbuf, gbuf, grecv).wait()

        def read(ref, e):
            pair = ref[e].astype(F32)
            return pair[:, :128], pair[:, 128:]

        tops = []
        for part, (ref, sign) in enumerate(((lbuf, 1), (gbuf, -1))):
            top = jnp.zeros((16, 128), F32)
            for r in range(4):
                pairs = [read(ref, 4 * a + r) for a in range(8)]
                for v in pairs:
                    top = jnp.maximum(top, jnp.maximum(jnp.abs(v[0]), jnp.abs(v[1])))
                out = fft(pairs, sign)
                for s, v in enumerate(out):
                    v = turn(v, sign * r * s, 32)
                    work[part, 4 * s + r, :, :128] = v[0]
                    work[part, 4 * s + r, :, 128:] = v[1]
            tops.append(jnp.max(jnp.max(top, axis=0, keepdims=True), axis=1, keepdims=True))
        bound = jnp.maximum(tops[0] * tops[1] * MARGIN, 2.0**-90)
        scale = 1.0 / (n_energy * bound)
        bound_out[...] = jnp.broadcast_to(bound, (1, 128))

        for s in range(8):
            hats = []
            for part, sign in ((0, 1), (1, -1)):
                pairs = [
                    (work[part, 4 * s + r, :, :128], work[part, 4 * s + r, :, 128:]) for r in range(4)
                ]
                hats.append(fft(pairs, sign))
            prods = [
                (a[0] * b[0] - a[1] * b[1], a[0] * b[1] + a[1] * b[0]) for a, b in zip(*hats)
            ]
            for r, v in enumerate(fft(prods, -1)):
                v = turn(v, -r * s, 32)
                wide[8 * r + s, :, :128] = v[0]
                wide[8 * r + s, :, 128:] = v[1]
        for r in range(4):
            pairs = [(wide[8 * r + s, :, :128], wide[8 * r + s, :, 128:]) for s in range(8)]
            for a, v in enumerate(fft(pairs, -1)):
                code[4 * a + r] = encode(jnp.concatenate(v, axis=1), scale).astype(jnp.bfloat16)

        def give(dest):
            @pl.when(dest != me)
            def _():
                pltpu.make_async_remote_copy(
                    bound_out, bound_in.at[unit_here], bsend.at[dest], brecv.at[unit_here],
                    device_id=(space, dest), device_id_type=MESH,
                ).start()
                pltpu.make_async_remote_copy(
                    code.at[dest], back.at[unit_here], psend.at[dest], precv.at[unit_here],
                    device_id=(space, dest), device_id_type=MESH,
                ).start()

            @pl.when(dest == me)
            def _():
                pltpu.make_async_copy(
                    bound_out, bound_in.at[unit_here], brecv.at[unit_here]
                ).start()
                pltpu.make_async_copy(code.at[dest], back.at[unit_here], precv.at[unit_here]).start()

        @pl.loop(0, 32)
        def _(k):
            give(k)

    @pl.loop(0, 24)
    def _(k):
        t, rows = unit_rows(k)
        pltpu.make_async_copy(bound_in.at[k], bound_in.at[k], brecv.at[k]).wait()
        pltpu.make_async_copy(back.at[k], back.at[k], precv.at[k]).wait()
        bound = jnp.concatenate([bound_in[k], bound_in[k]], axis=1)
        o_ref[0, 0, t, rows, :] = decode(back[k].astype(F32), bound)

    for copy in halos:
        copy.wait_send()

    @pl.loop(0, 16)
    def _(z):
        sent(lbuf, lsend, z, 0)
        sent(gbuf, gsend, z, 0)

        @pl.when(has_second(z))
        def _():
            sent(lbuf, lsend, z, 1)
            sent(gbuf, gsend, z, 1)

    @pl.when(works)
    def _():
        @pl.loop(1, n_energy)
        def _(k):
            dest = lax.rem(me + k, n_energy)
            pltpu.make_async_copy(code.at[dest], code.at[dest], psend.at[dest]).wait()
            pltpu.make_async_copy(bound_out, bound_out, bsend.at[dest]).wait()


def on_device(n_space, n_energy, lesser, greater):
    unit = (16, 256)
    dma = pltpu.SemaphoreType.DMA
    return pl.pallas_call(
        functools.partial(kernel, n_space, n_energy),
        out_shape=pltpu.VMEM(lesser.shape, F32),
        in_specs=[pl.BlockSpec(memory_space=pltpu.HBM)] * 2,
        out_specs=pl.BlockSpec(memory_space=pltpu.VMEM),
        scratch_shapes=[
            pltpu.VMEM((2, 128, 256), jnp.bfloat16),
            pltpu.VMEM((4, 128, 256), jnp.bfloat16),
            pltpu.VMEM((3, 128, 256), jnp.bfloat16),
            pltpu.VMEM((n_energy, *unit), jnp.bfloat16),
            pltpu.VMEM((n_energy, *unit), jnp.bfloat16),
            pltpu.VMEM((2, n_energy, *unit), F32),
            pltpu.VMEM((n_energy, *unit), F32),
            pltpu.VMEM((n_energy, *unit), jnp.bfloat16),
            pltpu.VMEM((24, *unit), jnp.bfloat16),
            pltpu.VMEM((1, 128), F32),
            pltpu.VMEM((24, 1, 128), F32),
            dma((2,)),
            dma((2,)),
            dma((2,)),
            dma((24,)),
            dma((24,)),
            dma,
            dma,
            dma((n_energy,)),
            dma((24,)),
            dma((n_energy,)),
            dma((24,)),
            pltpu.SemaphoreType.REGULAR((2,)),
            pltpu.SemaphoreType.REGULAR((2,)),
        ],
        compiler_params=pltpu.CompilerParams(
            collective_id=0, has_side_effects=True, vmem_limit_bytes=62 << 20
        ),
    )(lesser, greater)


def solution(mesh):
    spec = P("energy", "space", None, None, None)
    return jax.shard_map(
        functools.partial(on_device, mesh.shape["space"], mesh.shape["energy"]),
        mesh=mesh,
        in_specs=(spec, spec),
        out_specs=spec,
        check_vma=False,
    )
```

```python
import functools
import math

import jax
import jax.numpy as jnp
from jax import lax
from jax.experimental import pallas as pl
from jax.experimental.pallas import tpu as pltpu
from jax.sharding import PartitionSpec as P

MESH = pl.DeviceIdType.MESH
REACH, STEPS = 4, 1
F32 = jnp.float32

MARGIN = 64.2
STEEP, SHALLOW, KNEE = 13.2, 5.0, 10.0
TOP = 127.0
SHIFT = (STEEP - SHALLOW) * KNEE


def encode(value, scale):
    part = jnp.abs(value) * scale
    octave = jnp.log2(jnp.maximum(part, 2.0**-33))
    code = jnp.exp2(TOP + jnp.maximum(STEEP * octave, SHALLOW * octave - SHIFT))
    code = jnp.where(part < 2.0**-33, 0.0, code)
    return jnp.where(value < 0, -code, code)


def decode(code, bound):
    size = jnp.abs(code)
    level = jnp.log2(jnp.maximum(size, 2.0**-126)) - TOP
    octave = jnp.minimum(level * (1.0 / STEEP), (level + SHIFT) * (1.0 / SHALLOW))
    value = jnp.exp2(octave) * bound
    value = jnp.where(size == 0, 0.0, value)
    return jnp.where(code < 0, -value, value)


def cadd(a, b):
    return a[0] + b[0], a[1] + b[1]


def csub(a, b):
    return a[0] - b[0], a[1] - b[1]


def turn(a, step, total):
    step = step % total
    eighth = 8 * step
    re, im = a
    if eighth % total == 0:
        way = eighth // total
        if way % 2 == 0:
            return [(re, im), (im, -re), (-re, -im), (-im, re)][way // 2]
        half = math.sqrt(0.5)
        p, m = (re + im) * half, (im - re) * half
        return {1: (p, m), 3: (m, -p), 5: (-p, -m), 7: (-m, p)}[way]
    c = math.cos(2 * math.pi * step / total)
    s = math.sin(2 * math.pi * step / total)
    return re * c + im * s, im * c - re * s


def fft(values, sign):
    n = len(values)
    if n == 1:
        return values
    even, odd = fft(values[0::2], sign), fft(values[1::2], sign)
    odd = [turn(v, sign * k, n) for k, v in enumerate(odd)]
    return [cadd(a, b) for a, b in zip(even, odd)] + [csub(a, b) for a, b in zip(even, odd)]


def kernel(
    n_space, n_energy,
    l_ref, g_ref, o_ref,
    halo, local, mirror, lbuf, gbuf, work, wide, code, back, bound_out, bound_in,
    own_sem, halo_send, halo_recv, lsend, gsend, lrecv, grecv, psend, precv, bsend, brecv, from_behind, from_ahead,
):
    space, me = lax.axis_index("space"), lax.axis_index("energy")
    core = lax.rem(space, 2)
    plane, side = me // 2, lax.rem(me, 2)
    up, down = lax.rem(space + 1, n_space), lax.rem(space + n_space - 1, n_space)

    first = side == lax.rem(plane + core, 2)
    rest = lax.rem(plane, 4) - 2 * core
    second = jnp.logical_and(jnp.logical_not(first), jnp.logical_or(rest == 0, rest == 1))
    unit_here = jnp.where(first, plane, 16 + 2 * (plane // 4) + rest)
    works = jnp.logical_or(first, second)

    l_copy = pltpu.make_async_copy(l_ref.at[0, 0], local.at[pl.ds(0, 3)], own_sem.at[0])
    own_copy = pltpu.make_async_copy(g_ref.at[0, 0, 1], local.at[3], own_sem.at[1])
    l_copy.start()
    own_copy.start()
    barrier = pltpu.get_barrier_semaphore()
    pl.semaphore_signal(barrier, inc=1, device_id=(up, me), device_id_type=MESH)
    pl.semaphore_signal(barrier, inc=1, device_id=(down, me), device_id_type=MESH)


    @pl.loop(0, 2 * (2 * REACH + 1))
    def _(k):
        peer = lax.rem(2 * plane + n_energy - 2 * REACH + k, n_energy)

        @pl.when(peer != me)
        def _():
            pl.semaphore_signal(barrier, inc=1, device_id=(space, peer), device_id_type=MESH)

    ahead = (space, lax.rem(me + 2 * REACH, n_energy))
    behind = (space, lax.rem(me + n_energy - 2 * REACH, n_energy))

    def flipped(tile):
        tile = tile.astype(F32)
        return jnp.concatenate([tile[:, :128].T, tile[:, 128:].T], axis=1)

    pl.semaphore_wait(barrier, 2 * (2 * REACH + 1) + 1)

    def tell(sem, peer):
        pl.semaphore_signal(sem, inc=1, device_id=peer, device_id_type=MESH)

    tell(from_behind.at[1], ahead)
    tell(from_ahead.at[1], behind)

    halos = [
        pltpu.make_async_remote_copy(
            g_ref.at[0, 0, 2 - 2 * i], halo.at[i], halo_send.at[i], halo_recv.at[i],
            device_id=(dest, me), device_id_type=MESH,
        )
        for i, dest in ((0, up), (1, down))
    ]
    for copy in halos:
        copy.start()

    def unit_rows(unit):
        return unit // 8, pl.ds(pl.multiple_of(lax.rem(unit, 8) * 16, 16), 16)

    def plane_at(k):
        away = 8 + jnp.where(lax.rem(k, 2) == 0, k // 2, -((k + 1) // 2))
        return lax.rem(plane + away, 16)

    def has_second(z):
        late = lax.rem(z, 4) - 2 * core
        return jnp.logical_or(late == 0, late == 1)

    def unit_of(z, which):
        return z if which == 0 else 16 + 2 * (z // 4) + lax.rem(lax.rem(z, 4), 2)

    def owner_of(z, which):
        return 2 * z + lax.rem(lax.rem(z, 2) + core + which, 2)

    def send(source, target, sems, recv, z, which):
        unit, dest = unit_of(z, which), owner_of(z, which)
        t, rows = unit_rows(unit)

        @pl.when(dest != me)
        def _():
            pltpu.make_async_remote_copy(
                source.at[t, rows], target.at[me], sems.at[unit], recv,
                device_id=(space, dest), device_id_type=MESH,
            ).start()

        @pl.when(dest == me)
        def _():
            pltpu.make_async_copy(source.at[t, rows], target.at[me], recv).start()

    def sent(source, sems, z, which):
        @pl.when(owner_of(z, which) != me)
        def _():
            pltpu.make_async_copy(source.at[0], source.at[0], sems.at[unit_of(z, which)]).wait()

    l_copy.wait()

    def send_lesser(z):
        send(local, lbuf, lsend, lrecv, z, 0)

        @pl.when(has_second(z))
        def _():
            send(local, lbuf, lsend, lrecv, z, 1)

    def send_greater(z):
        send(mirror, gbuf, gsend, grecv, z, 0)

        @pl.when(has_second(z))
        def _():
            send(mirror, gbuf, gsend, grecv, z, 1)

    def around(act, distances):
        for k in distances:
            act(lax.rem(plane + 16 - k, 16))
            if k % 8:
                act(lax.rem(plane + k, 16))

    def hear(step):
        for sem, peer in ((from_behind, ahead), (from_ahead, behind)):
            pl.semaphore_wait(sem.at[step], 1)
            if step < STEPS:
                tell(sem.at[step + 1], peer)

    around(send_lesser, (4, 3, 2, 1, 0))
    hear(1)
    around(send_lesser, (8, 7, 6, 5))
    own_copy.wait()
    mirror[1] = flipped(local[3]).astype(jnp.bfloat16)
    halos[0].wait_recv()
    left = flipped(halo[0])
    mirror[0] = jnp.where(space > 0, left, 0.0).astype(jnp.bfloat16)
    halos[1].wait_recv()
    right = flipped(halo[1])
    mirror[2] = jnp.where(space < n_space - 1, right, 0.0).astype(jnp.bfloat16)
    around(send_greater, (8, 7, 6, 5, 4, 3, 2, 1, 0))

    @pl.when(works)
    def _():
        pltpu.make_async_copy(lbuf, lbuf, lrecv).wait()
        pltpu.make_async_copy(gbuf, gbuf, grecv).wait()

        def read(ref, e):
            pair = ref[e].astype(F32)
            return pair[:, :128], pair[:, 128:]

        tops = []
        for part, (ref, sign) in enumerate(((lbuf, 1), (gbuf, -1))):
            top = jnp.zeros((16, 128), F32)
            for r in range(4):
                pairs = [read(ref, 4 * a + r) for a in range(8)]
                for v in pairs:
                    top = jnp.maximum(top, jnp.maximum(jnp.abs(v[0]), jnp.abs(v[1])))
                out = fft(pairs, sign)
                for s, v in enumerate(out):
                    v = turn(v, sign * r * s, 32)
                    work[part, 4 * s + r, :, :128] = v[0]
                    work[part, 4 * s + r, :, 128:] = v[1]
            tops.append(jnp.max(jnp.max(top, axis=0, keepdims=True), axis=1, keepdims=True))
        bound = jnp.maximum(tops[0] * tops[1] * MARGIN, 2.0**-90)
        scale = 1.0 / (n_energy * bound)
        bound_out[...] = jnp.broadcast_to(bound, (1, 128))

        for s in range(8):
            hats = []
            for part, sign in ((0, 1), (1, -1)):
                pairs = [
                    (work[part, 4 * s + r, :, :128], work[part, 4 * s + r, :, 128:]) for r in range(4)
                ]
                hats.append(fft(pairs, sign))
            prods = [
                (a[0] * b[0] - a[1] * b[1], a[0] * b[1] + a[1] * b[0]) for a, b in zip(*hats)
            ]
            for r, v in enumerate(fft(prods, -1)):
                v = turn(v, -r * s, 32)
                wide[8 * r + s, :, :128] = v[0]
                wide[8 * r + s, :, 128:] = v[1]
        for r in range(4):
            pairs = [(wide[8 * r + s, :, :128], wide[8 * r + s, :, 128:]) for s in range(8)]
            for a, v in enumerate(fft(pairs, -1)):
                code[4 * a + r] = encode(jnp.concatenate(v, axis=1), scale).astype(jnp.bfloat16)

        def give(dest):
            @pl.when(dest != me)
            def _():
                pltpu.make_async_remote_copy(
                    bound_out, bound_in.at[unit_here], bsend.at[dest], brecv.at[unit_here],
                    device_id=(space, dest), device_id_type=MESH,
                ).start()
                pltpu.make_async_remote_copy(
                    code.at[dest], back.at[unit_here], psend.at[dest], precv.at[unit_here],
                    device_id=(space, dest), device_id_type=MESH,
                ).start()

            @pl.when(dest == me)
            def _():
                pltpu.make_async_copy(
                    bound_out, bound_in.at[unit_here], brecv.at[unit_here]
                ).start()
                pltpu.make_async_copy(code.at[dest], back.at[unit_here], precv.at[unit_here]).start()

        def given(dest):
            @pl.when(dest != me)
            def _():
                pltpu.make_async_copy(code.at[dest], code.at[dest], psend.at[dest]).wait()

        @pl.loop(0, 32)
        def _(k):
            @pl.when(jnp.logical_and(core == 1, k >= 12))
            def _():
                given(k - 12)

            give(k)

    @pl.loop(0, 24)
    def _(k):
        t, rows = unit_rows(k)
        pltpu.make_async_copy(bound_in.at[k], bound_in.at[k], brecv.at[k]).wait()
        pltpu.make_async_copy(back.at[k], back.at[k], precv.at[k]).wait()
        bound = jnp.concatenate([bound_in[k], bound_in[k]], axis=1)
        o_ref[0, 0, t, rows, :] = decode(back[k].astype(F32), bound)

    for copy in halos:
        copy.wait_send()

    @pl.loop(0, 16)
    def _(z):
        sent(lbuf, lsend, z, 0)
        sent(gbuf, gsend, z, 0)

        @pl.when(has_second(z))
        def _():
            sent(lbuf, lsend, z, 1)
            sent(gbuf, gsend, z, 1)

    @pl.when(works)
    def _():
        @pl.loop(1, n_energy)
        def _(k):
            dest = lax.rem(me + k, n_energy)
            @pl.when(jnp.logical_or(core == 0, dest >= 20))
            def _():
                pltpu.make_async_copy(code.at[dest], code.at[dest], psend.at[dest]).wait()

            pltpu.make_async_copy(bound_out, bound_out, bsend.at[dest]).wait()


def on_device(n_space, n_energy, lesser, greater):
    unit = (16, 256)
    dma = pltpu.SemaphoreType.DMA
    return pl.pallas_call(
        functools.partial(kernel, n_space, n_energy),
        out_shape=pltpu.VMEM(lesser.shape, F32),
        in_specs=[pl.BlockSpec(memory_space=pltpu.HBM)] * 2,
        out_specs=pl.BlockSpec(memory_space=pltpu.VMEM),
        scratch_shapes=[
            pltpu.VMEM((2, 128, 256), jnp.bfloat16),
            pltpu.VMEM((4, 128, 256), jnp.bfloat16),
            pltpu.VMEM((3, 128, 256), jnp.bfloat16),
            pltpu.VMEM((n_energy, *unit), jnp.bfloat16),
            pltpu.VMEM((n_energy, *unit), jnp.bfloat16),
            pltpu.VMEM((2, n_energy, *unit), F32),
            pltpu.VMEM((n_energy, *unit), F32),
            pltpu.VMEM((n_energy, *unit), jnp.bfloat16),
            pltpu.VMEM((24, *unit), jnp.bfloat16),
            pltpu.VMEM((1, 128), F32),
            pltpu.VMEM((24, 1, 128), F32),
            dma((2,)),
            dma((2,)),
            dma((2,)),
            dma((24,)),
            dma((24,)),
            dma,
            dma,
            dma((n_energy,)),
            dma((24,)),
            dma((n_energy,)),
            dma((24,)),
            pltpu.SemaphoreType.REGULAR((2,)),
            pltpu.SemaphoreType.REGULAR((2,)),
        ],
        compiler_params=pltpu.CompilerParams(
            collective_id=0, has_side_effects=True, vmem_limit_bytes=62 << 20
        ),
    )(lesser, greater)


def solution(mesh):
    spec = P("energy", "space", None, None, None)
    return jax.shard_map(
        functools.partial(on_device, mesh.shape["space"], mesh.shape["energy"]),
        mesh=mesh,
        in_specs=(spec, spec),
        out_specs=spec,
        check_vma=False,
    )
```
